32 devices in a mesh: gx: 4 (over y, core), gy: 8 (over z, x).
Axes of the slice: x: 2, y: 2, z: 4, core: 2. Of those that a mesh axis runs over, the one named last changes fastest.
Arguments:
- tokens: bfloat16 [2, 256, 8192], P(None, None, 'gy'), may hold values from -64 to 64
- cache_lengths: int32 [256], P('gy'), may hold values from 128 to 1024, as said below
- key_cache: bfloat16 [256, 1024, 8, 128], P('gy', None, 'gx'), may hold values from -128 to 128
- value_cache: bfloat16 [256, 1024, 8, 128], P('gy', None, 'gx'), may hold values from -6 to 6
- attn_gain: bfloat16 [8192], P('gy'), may hold values from 0.5 to 1.5
- query_weight: bfloat16 [8192, 8192], P('gy', 'gx'), may hold values from -0.0625 to 0.0625
- keyval_weight: bfloat16 [8192, 2048], P('gy', 'gx'), may hold values from -0.0625 to 0.0625
- out_weight: bfloat16 [8192, 8192], P('gx', 'gy'), may hold values from -0.25 to 0.25
- ffn_gain: bfloat16 [8192], P('gy'), may hold values from 0.5 to 1.5
- gate_weight: bfloat16 [8192, 14336], P('gy', 'gx'), may hold values from -0.0625 to 0.0625
- up_weight: bfloat16 [8192, 14336], P('gy', 'gx'), may hold values from -0.0625 to 0.0625
- down_weight: bfloat16 [14336, 8192], P('gx', 'gy'), may hold values from -0.046875 to 0.046875
Outputs:
- layer_out: bfloat16 [2, 256, 8192], P(None, None, 'gy')
The draws below stay inside these ranges and needn't reach their ends.
Inputs may be any that keep to these rules, and one draw needn't show every extreme that they name: `cache_lengths`: some sequence has exactly 1024 cached tokens.
All inputs are finite; a program needn't handle non-finite values.
Results may differ from the reference program's by a relative error of at most 0.0095.
Values may be sent and summed in bfloat16 or wider, within the bound.
A program may use at most 192 MiB of HBM per device.

```python
import math
import jax
import jax.numpy as jnp
from jax import lax

D = 8192
QH = 64
KVH = 8
HD = 128
FF = 14336
MAXLEN = 1024
GROUP = 8
SEQS = 256
LEN_MIN = 128


def draw_tokens(key, part):
    key = jax.random.fold_in(key, 11)
    keys = jax.random.split(key, 3)
    column = jnp.arange(D, dtype=jnp.float32) / D
    shape = (2, SEQS, D)
    base = jax.random.normal(keys[0], shape, jnp.float32)
    ramp = jnp.sqrt(1.0 + 2.0 * column)
    jitter = jnp.exp(jax.random.uniform(keys[1], (D,), jnp.float32, -0.4, 0.4))
    scales = jnp.exp(jax.random.uniform(keys[2], (2, SEQS, 1), jnp.float32, math.log(0.5), math.log(2.0)))
    return jnp.clip(base * ramp * jitter * scales, -64.0, 64.0).astype(jnp.bfloat16)


def draw_cache_lengths(key, part):
    key = jax.random.fold_in(key, 23)
    draw_key, spot_key = jax.random.split(key)
    drawn = jax.random.randint(draw_key, (SEQS,), LEN_MIN, MAXLEN + 1)
    longest = jax.random.randint(spot_key, (), 0, SEQS)
    return jnp.where(jnp.arange(SEQS) == longest, MAXLEN, drawn).astype(jnp.int32)


def draw_key_cache(key, part):
    key = jax.random.fold_in(key, 37)
    keys = jax.random.split(key, 1)
    shape = (SEQS, MAXLEN, KVH, HD)
    result = jnp.clip(jax.random.normal(keys[0], shape, jnp.float32), -6.0, 6.0)
    return result.astype(jnp.bfloat16)


def levels(rng, dims, pieces, least, top_value):
    level, own = 1.0, jax.random.fold_in(rng, 6)
    for axis_at, parts in pieces:
        draws = jnp.exp(jax.random.uniform(jax.random.fold_in(own, axis_at), (parts,), jnp.float32, least / len(pieces), top_value / len(pieces)))
        level = level * jnp.repeat(draws, dims[axis_at] // parts).reshape([-1 if axis == axis_at else 1 for axis in range(len(dims))])
    return level


def scatter_about(stream_key, dims, spread, reach, pieces=(), held_as=jnp.bfloat16):
    gain = levels(stream_key, dims, pieces, -0.22, 0.18) if pieces else 1.0
    values = jax.random.normal(stream_key, dims, jnp.float32) * spread * gain
    return jnp.minimum(jnp.maximum(values, -reach), reach).astype(held_as)


def setup_inputs(seed: int = 0) -> dict:
    seeds = jax.random.split(jax.random.key(seed), 13)
    tokens = draw_tokens(jax.random.fold_in(seeds[12], 71), 0)
    cache_lengths = draw_cache_lengths(jax.random.fold_in(seeds[12], 71), 0)
    key_cache = draw_key_cache(jax.random.fold_in(seeds[12], 71), 0)
    value_cache = scatter_about(seeds[3], (SEQS, MAXLEN, KVH, HD), 1.0, 6.0, ((0, 8), (2, 4)))
    attn_gain = jnp.clip(1.0 + 0.1 * jax.random.normal(seeds[4], (D,), jnp.float32), 0.5, 1.5).astype(jnp.bfloat16)
    query_weight = scatter_about(seeds[5], (D, QH * HD), D ** -0.5, 0.0625, ((0, 8), (1, 4)))
    keyval_weight = scatter_about(seeds[6], (D, 2 * KVH * HD), D ** -0.5, 0.0625, ((0, 8), (1, 4)))
    out_weight = scatter_about(seeds[7], (QH * HD, D), (QH * HD // 16) ** -0.5, 0.25, ((0, 4), (1, 8)))
    ffn_gain = jnp.clip(1.0 + 0.1 * jax.random.normal(seeds[8], (D,), jnp.float32), 0.5, 1.5).astype(jnp.bfloat16)
    gate_weight = scatter_about(seeds[9], (D, FF), D ** -0.5, 0.0625, ((0, 8), (1, 4)))
    up_weight = scatter_about(seeds[10], (D, FF), D ** -0.5, 0.0625, ((0, 8), (1, 4)))
    down_weight = scatter_about(seeds[11], (FF, D), FF ** -0.5, 0.046875, ((0, 4), (1, 8)))
    return {"tokens": tokens, "cache_lengths": cache_lengths, "key_cache": key_cache, "value_cache": value_cache, "attn_gain": attn_gain, "query_weight": query_weight, "keyval_weight": keyval_weight, "out_weight": out_weight, "ffn_gain": ffn_gain, "gate_weight": gate_weight, "up_weight": up_weight, "down_weight": down_weight}


epsilon = 1e-05
rotary_base = 500000.0

def rotary(values, positions):
    half_dim = HD // 2
    inv_freq = rotary_base ** (-(jnp.arange(half_dim, dtype=jnp.float32) * 2.0 / HD))
    angles = positions[:, None] * inv_freq[None, :]
    cosine = jnp.cos(angles)[:, None, :]
    sine_part = jnp.sin(angles)[:, None, :]
    first_half = values[..., :half_dim]
    second_half = values[..., half_dim:]
    return jnp.concatenate([first_half * cosine - second_half * sine_part, second_half * cosine + first_half * sine_part], axis=-1)

def attend_sequence(operands):
    queries, cached_keys, cached_values, length, extra_keys, extra_values = operands
    scale_factor = 1.0 / math.sqrt(HD)
    grouped = queries.astype(jnp.float32).reshape(KVH, GROUP, HD)
    cached = jnp.einsum('gjd,tgd->gjt', grouped, cached_keys.astype(jnp.float32)) * scale_factor
    valid = jnp.arange(MAXLEN) < length
    cached = jnp.where(valid[None, None, :], cached, -1e+30)
    recent = jnp.einsum('gjd,egd->gje', grouped, extra_keys.astype(jnp.float32)) * scale_factor
    highest = jnp.maximum(lax.optimization_barrier(jnp.max(cached, axis=-1, keepdims=True)), lax.optimization_barrier(jnp.max(recent, axis=-1, keepdims=True)))
    cached_exp = jnp.exp(cached - highest)
    recent_exp = jnp.exp(recent - highest)
    totals = lax.optimization_barrier(jnp.sum(cached_exp, axis=-1, keepdims=True)) + lax.optimization_barrier(jnp.sum(recent_exp, axis=-1, keepdims=True))
    cached_probs = (cached_exp / totals).astype(jnp.bfloat16)
    recent_probs = (recent_exp / totals).astype(jnp.bfloat16)
    mixed = jnp.einsum('gjt,tgd->gjd', cached_probs.astype(jnp.float32), cached_values.astype(jnp.float32))
    mixed = mixed + jnp.einsum('gje,egd->gjd', recent_probs.astype(jnp.float32), extra_values.astype(jnp.float32))
    return mixed.reshape(QH, HD).astype(jnp.bfloat16)

def reference(tokens, cache_lengths, key_cache, value_cache, attn_gain, query_weight, keyval_weight, out_weight, ffn_gain, gate_weight, up_weight, down_weight):
    results = []
    keys_new = []
    values_new = []
    for decode_step in range(2):
        current = tokens[decode_step].astype(jnp.float32)
        attn_ms = lax.optimization_barrier(jnp.mean(current * current, axis=1, keepdims=True))
        normed = (current * lax.rsqrt(attn_ms + epsilon) * attn_gain.astype(jnp.float32)).astype(jnp.bfloat16)
        query_part = jnp.dot(normed, query_weight, preferred_element_type=jnp.float32).reshape(SEQS, QH, HD)
        key_value = jnp.dot(normed, keyval_weight, preferred_element_type=jnp.float32).reshape(SEQS, KVH, 2, HD)
        positions = (cache_lengths + decode_step).astype(jnp.float32)
        queries = rotary(query_part, positions).astype(jnp.bfloat16)
        keys_new.append(rotary(key_value[:, :, 0], positions).astype(jnp.bfloat16))
        values_new.append(key_value[:, :, 1].astype(jnp.bfloat16))
        extra_keys = jnp.stack(keys_new, axis=1)
        extra_values = jnp.stack(values_new, axis=1)
        attended = lax.map(attend_sequence, (queries, key_cache, value_cache, cache_lengths, extra_keys, extra_values))
        attended = attended.reshape(SEQS, QH * HD)
        projected = jnp.dot(attended, out_weight, preferred_element_type=jnp.float32)
        resid = (current + projected).astype(jnp.bfloat16)
        resid_f = resid.astype(jnp.float32)
        ffn_ms = lax.optimization_barrier(jnp.mean(resid_f * resid_f, axis=1, keepdims=True))
        ffn_in = (resid_f * lax.rsqrt(ffn_ms + epsilon) * ffn_gain.astype(jnp.float32)).astype(jnp.bfloat16)
        gate_sum = jnp.dot(ffn_in, gate_weight, preferred_element_type=jnp.float32)
        up_sum = jnp.dot(ffn_in, up_weight, preferred_element_type=jnp.float32)
        activated = (jax.nn.silu(gate_sum) * up_sum).astype(jnp.bfloat16)
        down_sum = jnp.dot(activated, down_weight, preferred_element_type=jnp.float32)
        results.append((resid_f + down_sum).astype(jnp.bfloat16))
    return jnp.stack(results)
```

```python
import functools
import math

import jax
import jax.numpy as jnp
from jax import lax
from jax.experimental import pallas as pl
from jax.experimental.pallas import tpu as pltpu
from jax.sharding import PartitionSpec as P

HD = 128
GROUP = 8
EXTRA = 128
VMEM_LIMIT = 56 * 1024 * 1024
MESH = pl.DeviceIdType.MESH

epsilon = 1e-05
rotary_base = 500000.0


def remote(src, dst, send, recv, axis, device):
    return pltpu.make_async_remote_copy(
        src_ref=src,
        dst_ref=dst,
        send_sem=send,
        recv_sem=recv,
        device_id={axis: device},
        device_id_type=MESH,
    )


def enter(axis, peers):
    barrier = pltpu.get_barrier_semaphore()
    for peer in peers:
        pl.semaphore_signal(barrier, inc=1, device_id={axis: peer}, device_id_type=MESH)
    pl.semaphore_wait(barrier, len(peers))


def scatter_kernel(n, parts, p_ref, out_ref, near, going, far, ns, nr, fs, fr):
    outer = n // 2
    me = lax.axis_index("gy")
    o, i = me // 2, lax.rem(me, 2)
    partner = me + 1 - 2 * i
    across = [lax.rem(o + k, outer) for k in range(outer)]
    enter("gy", [partner] + [across[k] * 2 + i for k in range(1, outer)])
    width = p_ref.shape[2] // parts
    order = [(s, (k + 1) % outer) for s in range(parts) for k in range(outer)]
    near_copies, far_copies = [], []

    def start_near(s, k):
        cols = pl.ds(s * width, width)
        copy = remote(
            p_ref.at[across[k] * 2 + 1 - i, :, cols],
            near.at[k, :, cols],
            ns.at[s, k],
            nr.at[s, k],
            "gy",
            partner,
        )
        copy.start()
        near_copies.append(copy)

    window = 3
    for s, k in order[:window]:
        start_near(s, k)
    for j, (s, k) in enumerate(order):
        cols = pl.ds(s * width, width)
        near_copies[j].wait_recv()
        near_copies[j].wait_send()
        if j + window < len(order):
            start_near(*order[j + window])
        total = p_ref[across[k] * 2 + i, :, cols].astype(jnp.float32) + near[k, :, cols].astype(
            jnp.float32
        )
        if k == 0:
            out_ref[:, cols] = total
        else:
            going[k - 1, :, cols] = total.astype(jnp.bfloat16)
            copy = remote(
                going.at[k - 1, :, cols],
                far.at[k - 1, :, cols],
                fs.at[s, k - 1],
                fr.at[s, k - 1],
                "gy",
                across[k] * 2 + i,
            )
            copy.start()
            far_copies.append((s, k, copy))
    for s in range(parts):
        cols = pl.ds(s * width, width)
        total = out_ref[:, cols]
        for cs, k, copy in far_copies:
            if cs == s:
                copy.wait_recv()
                total = total + far[k - 1, :, cols].astype(jnp.float32)
        out_ref[:, cols] = total
    for _, _, copy in far_copies:
        copy.wait_send()


def scatter_sum(partial, n, collective_id):
    _, rows, cols = partial.shape
    outer = n // 2
    parts = 3 if cols % 384 == 0 else 1
    return pl.pallas_call(
        functools.partial(scatter_kernel, n, parts),
        out_shape=jax.ShapeDtypeStruct((rows, cols), jnp.float32),
        in_specs=[pl.BlockSpec(memory_space=pltpu.VMEM)],
        out_specs=pl.BlockSpec(memory_space=pltpu.VMEM),
        scratch_shapes=[
            pltpu.VMEM((outer, rows, cols), jnp.bfloat16),
            pltpu.VMEM((outer - 1, rows, cols), jnp.bfloat16),
            pltpu.VMEM((outer - 1, rows, cols), jnp.bfloat16),
            pltpu.SemaphoreType.DMA((parts, outer)),
            pltpu.SemaphoreType.DMA((parts, outer)),
            pltpu.SemaphoreType.DMA((parts, outer - 1)),
            pltpu.SemaphoreType.DMA((parts, outer - 1)),
        ],
        compiler_params=pltpu.CompilerParams(
            collective_id=collective_id, has_side_effects=True, vmem_limit_bytes=VMEM_LIMIT
        ),
    )(partial)


def gather_kernel(n, a_ref, out_ref, own, ns, nr, fs, fr):
    outer = n // 2
    me = lax.axis_index("gy")
    o, i = me // 2, lax.rem(me, 2)
    partner = me + 1 - 2 * i
    across = [lax.rem(o + k, outer) * 2 + i for k in range(outer)]
    behind = [lax.rem(o + outer - k, outer) * 2 + i for k in range(outer)]
    enter("gy", [partner] + across[1:])
    far_copies, near_copies = [], []
    for k in range(1, outer):
        copy = remote(a_ref, out_ref.at[me], fs.at[k - 1], fr.at[k - 1], "gy", across[k])
        copy.start()
        far_copies.append(copy)
    copy = remote(a_ref, out_ref.at[me], ns.at[0], nr.at[0], "gy", partner)
    copy.start()
    near_copies.append(copy)
    mine = pltpu.make_async_copy(a_ref, out_ref.at[me], own)
    mine.start()
    for k in range(1, outer):
        far_copies[k - 1].wait_recv()
        block = out_ref.at[behind[k]]
        copy = remote(block, block, ns.at[k], nr.at[k], "gy", partner)
        copy.start()
        near_copies.append(copy)
    for copy in near_copies:
        copy.wait_recv()
    for copy in far_copies + near_copies:
        copy.wait_send()
    mine.wait()


def gather_rows(block, n, collective_id):
    rows, cols = block.shape
    outer = n // 2
    return pl.pallas_call(
        functools.partial(gather_kernel, n),
        out_shape=jax.ShapeDtypeStruct((n, rows, cols), block.dtype),
        in_specs=[pl.BlockSpec(memory_space=pltpu.VMEM)],
        out_specs=pl.BlockSpec(memory_space=pltpu.VMEM),
        scratch_shapes=[
            pltpu.SemaphoreType.DMA,
            pltpu.SemaphoreType.DMA((outer,)),
            pltpu.SemaphoreType.DMA((outer,)),
            pltpu.SemaphoreType.DMA((outer - 1,)),
            pltpu.SemaphoreType.DMA((outer - 1,)),
        ],
        compiler_params=pltpu.CompilerParams(
            collective_id=collective_id, has_side_effects=True, vmem_limit_bytes=VMEM_LIMIT
        ),
    )(block)


def residual_kernel(n, p_ref, base_ref, out_ref, got, ss, sr, gs, gr):
    me = lax.axis_index("gx")
    across = [lax.rem(me + k, n) for k in range(n)]
    enter("gx", across[1:])
    sums, shares = [], []
    for k in range(1, n):
        copy = remote(
            p_ref.at[across[k]], got.at[k - 1], ss.at[k - 1], sr.at[k - 1], "gx", across[k]
        )
        copy.start()
        sums.append(copy)
    total = p_ref[me].astype(jnp.float32)
    for k in range(1, n):
        sums[k - 1].wait_recv()
        total = total + got[k - 1].astype(jnp.float32)
    out_ref[me] = (base_ref[me].astype(jnp.float32) + total).astype(jnp.bfloat16)
    for k in range(1, n):
        copy = remote(
            out_ref.at[me], out_ref.at[me], gs.at[k - 1], gr.at[k - 1], "gx", across[k]
        )
        copy.start()
        shares.append(copy)
    for copy in shares:
        copy.wait_recv()
    for copy in sums + shares:
        copy.wait_send()


def add_residual(partial, base, n, collective_id):
    rows, cols = partial.shape
    shape = (n, rows // n, cols)
    result = pl.pallas_call(
        functools.partial(residual_kernel, n),
        out_shape=jax.ShapeDtypeStruct(shape, jnp.bfloat16),
        in_specs=[pl.BlockSpec(memory_space=pltpu.VMEM)] * 2,
        out_specs=pl.BlockSpec(memory_space=pltpu.VMEM),
        scratch_shapes=[pltpu.VMEM((n - 1,) + shape[1:], jnp.bfloat16)]
        + [pltpu.SemaphoreType.DMA((n - 1,))] * 4,
        compiler_params=pltpu.CompilerParams(
            collective_id=collective_id, has_side_effects=True, vmem_limit_bytes=VMEM_LIMIT
        ),
    )(partial.reshape(shape), base.reshape(shape))
    return result.reshape(rows, cols)


def rotary(values, positions):
    half_dim = HD // 2
    inv_freq = rotary_base ** (-(jnp.arange(half_dim, dtype=jnp.float32) * 2.0 / HD))
    angles = positions[..., None] * inv_freq
    cosine = jnp.cos(angles)[..., None, :]
    sine_part = jnp.sin(angles)[..., None, :]
    first_half = values[..., :half_dim]
    second_half = values[..., half_dim:]
    return jnp.concatenate(
        [
            first_half * cosine - second_half * sine_part,
            second_half * cosine + first_half * sine_part,
        ],
        axis=-1,
    )


def attend(queries, cached_keys, cached_values, lengths, extra_keys, extra_values):
    seqs, kv, steps = queries.shape[:3]
    flat = queries.reshape(seqs, kv, steps * GROUP, HD)
    scale_factor = 1.0 / math.sqrt(HD)
    cached = (
        jnp.einsum("sgjd,stgd->sgjt", flat, cached_keys, preferred_element_type=jnp.float32)
        * scale_factor
    )
    valid = jnp.arange(cached_keys.shape[1])[None, :] < lengths[:, None]
    cached = jnp.where(valid[:, None, None, :], cached, -1e30)
    recent = (
        jnp.einsum("sgjd,segd->sgje", flat, extra_keys, preferred_element_type=jnp.float32)
        * scale_factor
    )
    step_of = jnp.arange(steps * GROUP) // GROUP
    seen = jnp.arange(steps)[None, :] <= step_of[:, None]
    recent = jnp.where(seen[None, None], recent, -1e30)
    highest = jnp.maximum(
        jnp.max(cached, axis=-1, keepdims=True), jnp.max(recent, axis=-1, keepdims=True)
    )
    cached_exp = jnp.exp(cached - highest)
    recent_exp = jnp.exp(recent - highest)
    totals = jnp.sum(cached_exp, axis=-1, keepdims=True) + jnp.sum(
        recent_exp, axis=-1, keepdims=True
    )
    cached_probs = (cached_exp / totals).astype(jnp.bfloat16)
    recent_probs = (recent_exp / totals).astype(jnp.bfloat16)
    mixed = jnp.einsum(
        "sgjt,stgd->sgjd", cached_probs, cached_values, preferred_element_type=jnp.float32
    )
    mixed = mixed + jnp.einsum(
        "sgje,segd->sgjd", recent_probs, extra_values, preferred_element_type=jnp.float32
    )
    return mixed.reshape(seqs, kv, steps, GROUP, HD).astype(jnp.bfloat16)


def gained(values, gain):
    wide = values.astype(jnp.float32)
    squares = jnp.sum(wide * wide, axis=1, keepdims=True)
    high = squares.astype(jnp.bfloat16)
    low = (squares - high.astype(jnp.float32)).astype(jnp.bfloat16)
    pad = jnp.zeros((values.shape[0], EXTRA - 2), jnp.bfloat16)
    return (wide * gain.astype(jnp.float32)).astype(jnp.bfloat16), [high, low, pad]


def project(values, weights, columns, n):
    parts = [
        jnp.dot(values, weight, preferred_element_type=jnp.float32).astype(jnp.bfloat16)
        for weight in weights
    ]
    return jnp.concatenate(parts + columns, axis=1).reshape(n, values.shape[0] // n, -1)


def row_scaled(summed, width):
    squares = summed[:, -EXTRA] + summed[:, 1 - EXTRA]
    return summed[:, :-EXTRA] * lax.rsqrt(squares / width + epsilon)[:, None]


def per_device(
    tokens,
    cache_lengths,
    key_cache,
    value_cache,
    attn_gain,
    query_weight,
    keyval_weight,
    out_weight,
    ffn_gain,
    gate_weight,
    up_weight,
    down_weight,
):
    n, m = lax.axis_size("gy"), lax.axis_size("gx")
    steps, seqs, local = tokens.shape
    width = local * n
    seq_rows = cache_lengths.shape[0]
    query_cols = query_weight.shape[1]
    heads_local = query_cols // HD
    kv_local = keyval_weight.shape[1] // (2 * HD)
    hidden = gate_weight.shape[1]

    current = (
        tokens.reshape(steps, n, seq_rows, local).transpose(1, 0, 2, 3).reshape(steps * seqs, local)
    )
    values, columns = gained(current, attn_gain)
    projected = row_scaled(
        scatter_sum(project(values, [query_weight, keyval_weight], columns, n), n, 0), width
    )
    positions = (cache_lengths[None, :] + jnp.arange(steps)[:, None]).astype(jnp.float32)
    queries = rotary(
        projected[:, :query_cols].reshape(steps, seq_rows, heads_local, HD), positions
    ).astype(jnp.bfloat16)
    key_value = projected[:, query_cols:].reshape(steps, seq_rows, kv_local, 2, HD)
    new_keys = rotary(key_value[:, :, :, 0], positions).astype(jnp.bfloat16)
    new_values = key_value[:, :, :, 1].astype(jnp.bfloat16)
    attended = attend(
        queries.reshape(steps, seq_rows, kv_local, GROUP, HD).transpose(1, 2, 0, 3, 4),
        key_cache,
        value_cache,
        cache_lengths,
        new_keys.transpose(1, 0, 2, 3),
        new_values.transpose(1, 0, 2, 3),
    )
    attended = attended.transpose(2, 0, 1, 3, 4).reshape(steps * seq_rows, query_cols)
    gathered = gather_rows(attended, n, 1).reshape(steps * seqs, query_cols)
    partial_out = jnp.dot(gathered, out_weight, preferred_element_type=jnp.float32)
    resid = add_residual(partial_out.astype(jnp.bfloat16), current, m, 2)

    values, columns = gained(resid, ffn_gain)
    sums = row_scaled(
        scatter_sum(project(values, [gate_weight, up_weight], columns, n), n, 3), width
    )
    activated = (jax.nn.silu(sums[:, :hidden]) * sums[:, hidden:]).astype(jnp.bfloat16)
    gathered = gather_rows(activated, n, 4).reshape(steps * seqs, hidden)
    partial_down = jnp.dot(gathered, down_weight, preferred_element_type=jnp.float32)
    result = add_residual(partial_down.astype(jnp.bfloat16), resid, m, 5)
    return (
        result.reshape(n, steps, seq_rows, local).transpose(1, 0, 2, 3).reshape(steps, seqs, local)
    )


def solution(mesh):
    in_specs = (
        P(None, None, "gy"),
        P("gy"),
        P("gy", None, "gx", None),
        P("gy", None, "gx", None),
        P("gy"),
        P("gy", "gx"),
        P("gy", "gx"),
        P("gx", "gy"),
        P("gy"),
        P("gy", "gx"),
        P("gy", "gx"),
        P("gx", "gy"),
    )
    out_specs = P(None, None, "gy")
    return jax.shard_map(
        per_device, mesh=mesh, in_specs=in_specs, out_specs=out_specs, check_vma=False
    )
```

```python
import functools
import math

import jax
import jax.numpy as jnp
from jax import lax
from jax.experimental import pallas as pl
from jax.experimental.pallas import tpu as pltpu
from jax.sharding import PartitionSpec as P

HD = 128
GROUP = 8
EXTRA = 128
VMEM_LIMIT = 56 * 1024 * 1024
MESH = pl.DeviceIdType.MESH

epsilon = 1e-05
rotary_base = 500000.0


def remote(src, dst, send, recv, axis, device):
    return pltpu.make_async_remote_copy(
        src_ref=src,
        dst_ref=dst,
        send_sem=send,
        recv_sem=recv,
        device_id={axis: device},
        device_id_type=MESH,
    )


def enter(axis, peers):
    barrier = pltpu.get_barrier_semaphore()
    for peer in peers:
        pl.semaphore_signal(barrier, inc=1, device_id={axis: peer}, device_id_type=MESH)
    pl.semaphore_wait(barrier, len(peers))


def project_kernel(n, parts, gather, width, x_ref, sq_ref, w1_ref, w2_ref, *refs):
    if gather:
        out_ref, refs = refs[0], refs[1:]
    else:
        out1_ref, out2_ref, refs = refs[0], refs[1], refs[2:]
    w1, w2, p_ref, near, going, far, acc, scale, ws, ns, nr, fs, fr, as_, ar, bs, br = refs
    outer = n // 2
    me = lax.axis_index("gy")
    o, i = me // 2, lax.rem(me, 2)
    partner = me + 1 - 2 * i
    across = [lax.rem(o + k, outer) for k in range(outer)]
    behind = [lax.rem(o + outer - k, outer) * 2 + i for k in range(outer)]
    rows = sq_ref.shape[1]
    a, b = w1.shape[1] // parts, w2.shape[1] // parts
    size = a + b
    loads = []
    for s in range(parts):
        pair = []
        for j, (src, dst, c) in enumerate(((w1_ref, w1, a), (w2_ref, w2, b))):
            cols = pl.ds(s * c, c)
            copy = pltpu.make_async_copy(src.at[:, cols], dst.at[:, cols], ws.at[s, j])
            copy.start()
            pair.append(copy)
        loads.append(pair)
    enter("gy", [partner] + [across[k] * 2 + i for k in range(1, outer)])
    order = [(k + 1) % outer for k in range(outer)]
    segments = [(sq_ref, 0, parts * size, EXTRA)]
    segments += [(p_ref, s * size, s * size, size) for s in range(parts)]
    near_copies, far_copies, sent = {}, {}, []

    def near_start(g):
        src, start, place, count = segments[g]
        for k in order:
            copy = remote(
                src.at[across[k] * 2 + 1 - i, :, pl.ds(start, count)],
                near.at[k, :, pl.ds(place, count)],
                ns.at[g, k],
                nr.at[g, k],
                "gy",
                partner,
            )
            copy.start()
            near_copies[g, k] = copy

    def near_finish(g):
        src, start, place, count = segments[g]
        cols = pl.ds(place, count)
        for k in order:
            near_copies[g, k].wait_recv()
            sent.append(near_copies[g, k])
            total = src[across[k] * 2 + i, :, pl.ds(start, count)].astype(jnp.float32) + near[
                k, :, cols
            ].astype(jnp.float32)
            if k == 0:
                acc[:, cols] = total
            else:
                going[k - 1, :, cols] = total.astype(jnp.bfloat16)
                copy = remote(
                    going.at[k - 1, :, cols],
                    far.at[k - 1, :, cols],
                    fs.at[g, k - 1],
                    fr.at[g, k - 1],
                    "gy",
                    across[k] * 2 + i,
                )
                copy.start()
                far_copies[g, k] = copy

    def far_finish(g):
        place, count = segments[g][2:]
        cols = pl.ds(place, count)
        total = acc[:, cols]
        for k in range(1, outer):
            far_copies[g, k].wait_recv()
            sent.append(far_copies[g, k])
            total = total + far[k - 1, :, cols].astype(jnp.float32)
        return total

    share_far, share_near = {}, {}
    near_start(0)
    for t in range(parts + 3):
        if t < parts:
            for copy in loads[t]:
                copy.wait()
            x = x_ref[...]
            for buf, c, skip in ((w1, a, 0), (w2, b, a)):
                dot = jnp.dot(
                    x, buf[:, pl.ds(t * c, c)], preferred_element_type=jnp.float32
                ).astype(jnp.bfloat16)
                p_ref[:, :, pl.ds(t * size + skip, c)] = dot.reshape(n, rows, c)
            near_start(t + 1)
        if t == 0:
            near_finish(0)
        if 1 <= t <= parts:
            near_finish(t)
        if t == 1:
            squares = far_finish(0)
            scale[...] = jnp.broadcast_to(
                lax.rsqrt((squares[:, 0:1] + squares[:, 1:2]) / width + epsilon), scale.shape
            )
        if 2 <= t <= parts + 1:
            s = t - 2
            total = far_finish(s + 1) * scale[:, 0:1]
            if gather:
                cols = pl.ds(s * a, a)
                gate, up = total[:, :a], total[:, a:]
                out_ref[me, :, cols] = (gate / (1.0 + jnp.exp(-gate)) * up).astype(jnp.bfloat16)
                block = out_ref.at[me, :, cols]
                for k in range(1, outer):
                    copy = remote(
                        block, block, as_.at[s, k - 1], ar.at[s, k - 1], "gy", across[k] * 2 + i
                    )
                    copy.start()
                    share_far[s, k] = copy
                copy = remote(block, block, bs.at[s, 0], br.at[s, 0], "gy", partner)
                copy.start()
                share_near[s, 0] = copy
            else:
                out1_ref[:, pl.ds(s * a, a)] = total[:, :a]
                out2_ref[:, pl.ds(s * b, b)] = total[:, a:]
        if gather and t >= 3:
            s = t - 3
            cols = pl.ds(s * a, a)
            for k in range(1, outer):
                share_far[s, k].wait_recv()
                block = out_ref.at[behind[k], :, cols]
                copy = remote(block, block, bs.at[s, k], br.at[s, k], "gy", partner)
                copy.start()
                share_near[s, k] = copy
    for copy in share_near.values():
        copy.wait_recv()
    for copy in sent + list(share_far.values()) + list(share_near.values()):
        copy.wait_send()


def project(values, columns, weights, n, gather, collective_id):
    total_rows, depth = values.shape
    rows, outer = total_rows // n, n // 2
    c1, c2 = weights[0].shape[1], weights[1].shape[1]
    parts = max(p for p in range(1, 8) if c1 % (128 * p) == 0 and c2 % (128 * p) == 0)
    if gather:
        out_shape = jax.ShapeDtypeStruct((n, rows, c1), jnp.bfloat16)
        out_specs = pl.BlockSpec(memory_space=pltpu.VMEM)
    else:
        out_shape = [jax.ShapeDtypeStruct((rows, c), jnp.float32) for c in (c1, c2)]
        out_specs = [pl.BlockSpec(memory_space=pltpu.VMEM)] * 2
    cols = c1 + c2
    wide = cols + EXTRA
    dma = pltpu.SemaphoreType.DMA
    return pl.pallas_call(
        functools.partial(project_kernel, n, parts, gather, depth * n),
        out_shape=out_shape,
        in_specs=[pl.BlockSpec(memory_space=pltpu.VMEM)] * 2
        + [pl.BlockSpec(memory_space=pl.ANY)] * 2,
        out_specs=out_specs,
        scratch_shapes=[
            pltpu.VMEM((depth, c1), jnp.bfloat16),
            pltpu.VMEM((depth, c2), jnp.bfloat16),
            pltpu.VMEM((n, rows, cols), jnp.bfloat16),
            pltpu.VMEM((outer, rows, wide), jnp.bfloat16),
            pltpu.VMEM((outer - 1, rows, wide), jnp.bfloat16),
            pltpu.VMEM((outer - 1, rows, wide), jnp.bfloat16),
            pltpu.VMEM((rows, wide), jnp.float32),
            pltpu.VMEM((rows, 128), jnp.float32),
            dma((parts, 2)),
            dma((parts + 1, outer)),
            dma((parts + 1, outer)),
            dma((parts + 1, outer - 1)),
            dma((parts + 1, outer - 1)),
            dma((parts, outer - 1)),
            dma((parts, outer - 1)),
            dma((parts, outer)),
            dma((parts, outer)),
        ],
        compiler_params=pltpu.CompilerParams(
            collective_id=collective_id, has_side_effects=True, vmem_limit_bytes=VMEM_LIMIT
        ),
        cost_estimate=pl.CostEstimate(
            flops=2 * total_rows * depth * cols, bytes_accessed=2 * depth * cols, transcendentals=0
        ),
    )(values, columns.reshape(n, rows, EXTRA), *weights)


def gather_kernel(n, a_ref, out_ref, own, ns, nr, fs, fr):
    outer = n // 2
    me = lax.axis_index("gy")
    o, i = me // 2, lax.rem(me, 2)
    partner = me + 1 - 2 * i
    across = [lax.rem(o + k, outer) * 2 + i for k in range(outer)]
    behind = [lax.rem(o + outer - k, outer) * 2 + i for k in range(outer)]
    enter("gy", [partner] + across[1:])
    far_copies, near_copies = [], []
    for k in range(1, outer):
        copy = remote(a_ref, out_ref.at[me], fs.at[k - 1], fr.at[k - 1], "gy", across[k])
        copy.start()
        far_copies.append(copy)
    copy = remote(a_ref, out_ref.at[me], ns.at[0], nr.at[0], "gy", partner)
    copy.start()
    near_copies.append(copy)
    mine = pltpu.make_async_copy(a_ref, out_ref.at[me], own)
    mine.start()
    for k in range(1, outer):
        far_copies[k - 1].wait_recv()
        block = out_ref.at[behind[k]]
        copy = remote(block, block, ns.at[k], nr.at[k], "gy", partner)
        copy.start()
        near_copies.append(copy)
    for copy in near_copies:
        copy.wait_recv()
    for copy in far_copies + near_copies:
        copy.wait_send()
    mine.wait()


def gather_rows(block, n, collective_id):
    rows, cols = block.shape
    outer = n // 2
    return pl.pallas_call(
        functools.partial(gather_kernel, n),
        out_shape=jax.ShapeDtypeStruct((n, rows, cols), block.dtype),
        in_specs=[pl.BlockSpec(memory_space=pltpu.VMEM)],
        out_specs=pl.BlockSpec(memory_space=pltpu.VMEM),
        scratch_shapes=[
            pltpu.SemaphoreType.DMA,
            pltpu.SemaphoreType.DMA((outer,)),
            pltpu.SemaphoreType.DMA((outer,)),
            pltpu.SemaphoreType.DMA((outer - 1,)),
            pltpu.SemaphoreType.DMA((outer - 1,)),
        ],
        compiler_params=pltpu.CompilerParams(
            collective_id=collective_id, has_side_effects=True, vmem_limit_bytes=VMEM_LIMIT
        ),
    )(block)


def residual_kernel(n, p_ref, base_ref, out_ref, near, going, far, *sems):
    ns, nr, fs, fr, as_, ar, bs, br = sems
    outer = n // 2
    me = lax.axis_index("gx")
    o, i = me // 2, lax.rem(me, 2)
    partner = me + 1 - 2 * i
    across = [lax.rem(o + k, outer) for k in range(outer)]
    behind = [lax.rem(o + outer - k, outer) * 2 + i for k in range(outer)]
    enter("gx", [partner] + [across[k] * 2 + i for k in range(1, outer)])
    order = [(k + 1) % outer for k in range(outer)]
    copies, near_copies, far_copies, share_far, share_near = [], {}, {}, {}, {}

    def send(src, dst, send_sem, recv_sem, device):
        copy = remote(src, dst, send_sem, recv_sem, "gx", device)
        copy.start()
        copies.append(copy)
        return copy

    for k in order:
        near_copies[k] = send(
            p_ref.at[across[k] * 2 + 1 - i], near.at[k], ns.at[k], nr.at[k], partner
        )
    for k in order:
        near_copies[k].wait_recv()
        total = p_ref[across[k] * 2 + i].astype(jnp.float32) + near[k].astype(jnp.float32)
        if k:
            going[k - 1] = total.astype(jnp.bfloat16)
            far_copies[k] = send(
                going.at[k - 1],
                far.at[k - 1],
                fs.at[k - 1],
                fr.at[k - 1],
                across[k] * 2 + i,
            )
    for k in range(1, outer):
        far_copies[k].wait_recv()
        total = total + far[k - 1].astype(jnp.float32)
    out_ref[me] = (base_ref[me].astype(jnp.float32) + total).astype(jnp.bfloat16)
    block = out_ref.at[me]
    for k in range(1, outer):
        share_far[k] = send(block, block, as_.at[k - 1], ar.at[k - 1], across[k] * 2 + i)
    share_near[0] = send(block, block, bs.at[0], br.at[0], partner)
    for k in range(1, outer):
        share_far[k].wait_recv()
        block = out_ref.at[behind[k]]
        share_near[k] = send(block, block, bs.at[k], br.at[k], partner)
    for copy in share_near.values():
        copy.wait_recv()
    for copy in copies:
        copy.wait_send()


def add_residual(partial, base, n, collective_id):
    rows, cols = partial.shape
    shape = (n, rows // n, cols)
    outer = n // 2
    dma = pltpu.SemaphoreType.DMA
    result = pl.pallas_call(
        functools.partial(residual_kernel, n),
        out_shape=jax.ShapeDtypeStruct(shape, jnp.bfloat16),
        in_specs=[pl.BlockSpec(memory_space=pltpu.VMEM)] * 2,
        out_specs=pl.BlockSpec(memory_space=pltpu.VMEM),
        scratch_shapes=[
            pltpu.VMEM((outer,) + shape[1:], jnp.bfloat16),
            pltpu.VMEM((outer - 1,) + shape[1:], jnp.bfloat16),
            pltpu.VMEM((outer - 1,) + shape[1:], jnp.bfloat16),
        ]
        + [dma((outer,))] * 2
        + [dma((outer - 1,))] * 4
        + [dma((outer,))] * 2,
        compiler_params=pltpu.CompilerParams(
            collective_id=collective_id, has_side_effects=True, vmem_limit_bytes=VMEM_LIMIT
        ),
    )(partial.reshape(shape), base.reshape(shape))
    return result.reshape(rows, cols)


def rotary(values, positions):
    half_dim = HD // 2
    inv_freq = rotary_base ** (-(jnp.arange(half_dim, dtype=jnp.float32) * 2.0 / HD))
    angles = positions[..., None] * inv_freq
    cosine = jnp.cos(angles)[..., None, :]
    sine_part = jnp.sin(angles)[..., None, :]
    first_half = values[..., :half_dim]
    second_half = values[..., half_dim:]
    return jnp.concatenate(
        [
            first_half * cosine - second_half * sine_part,
            second_half * cosine + first_half * sine_part,
        ],
        axis=-1,
    )


def attend(queries, cached_keys, cached_values, lengths, extra_keys, extra_values):
    seqs, kv, steps = queries.shape[:3]
    flat = queries.reshape(seqs, kv, steps * GROUP, HD)
    scale_factor = 1.0 / math.sqrt(HD)
    cached = (
        jnp.einsum("sgjd,stgd->sgjt", flat, cached_keys, preferred_element_type=jnp.float32)
        * scale_factor
    )
    valid = jnp.arange(cached_keys.shape[1])[None, :] < lengths[:, None]
    cached = jnp.where(valid[:, None, None, :], cached, -1e30)
    recent = (
        jnp.einsum("sgjd,segd->sgje", flat, extra_keys, preferred_element_type=jnp.float32)
        * scale_factor
    )
    step_of = jnp.arange(steps * GROUP) // GROUP
    seen = jnp.arange(steps)[None, :] <= step_of[:, None]
    recent = jnp.where(seen[None, None], recent, -1e30)
    highest = jnp.maximum(
        jnp.max(cached, axis=-1, keepdims=True), jnp.max(recent, axis=-1, keepdims=True)
    )
    cached_exp = jnp.exp(cached - highest)
    recent_exp = jnp.exp(recent - highest)
    totals = jnp.sum(cached_exp, axis=-1, keepdims=True) + jnp.sum(
        recent_exp, axis=-1, keepdims=True
    )
    cached_probs = (cached_exp / totals).astype(jnp.bfloat16)
    recent_probs = (recent_exp / totals).astype(jnp.bfloat16)
    mixed = jnp.einsum(
        "sgjt,stgd->sgjd", cached_probs, cached_values, preferred_element_type=jnp.float32
    )
    mixed = mixed + jnp.einsum(
        "sgje,segd->sgjd", recent_probs, extra_values, preferred_element_type=jnp.float32
    )
    return mixed.reshape(seqs, kv, steps, GROUP, HD).astype(jnp.bfloat16)


def gained(values, gain):
    wide = values.astype(jnp.float32)
    squares = jnp.sum(wide * wide, axis=1, keepdims=True)
    high = squares.astype(jnp.bfloat16)
    low = (squares - high.astype(jnp.float32)).astype(jnp.bfloat16)
    pad = jnp.zeros((values.shape[0], EXTRA - 2), jnp.bfloat16)
    return (wide * gain.astype(jnp.float32)).astype(jnp.bfloat16), jnp.concatenate(
        [high, low, pad], axis=1
    )


def per_device(
    tokens,
    cache_lengths,
    key_cache,
    value_cache,
    attn_gain,
    query_weight,
    keyval_weight,
    out_weight,
    ffn_gain,
    gate_weight,
    up_weight,
    down_weight,
):
    n, m = lax.axis_size("gy"), lax.axis_size("gx")
    steps, seqs, local = tokens.shape
    seq_rows = cache_lengths.shape[0]
    query_cols = query_weight.shape[1]
    heads_local = query_cols // HD
    kv_local = keyval_weight.shape[1] // (2 * HD)
    hidden = gate_weight.shape[1]

    current = (
        tokens.reshape(steps, n, seq_rows, local).transpose(1, 0, 2, 3).reshape(steps * seqs, local)
    )
    values, columns = gained(current, attn_gain)
    query_part, key_value = project(values, columns, [query_weight, keyval_weight], n, False, 0)
    positions = (cache_lengths[None, :] + jnp.arange(steps)[:, None]).astype(jnp.float32)
    queries = rotary(
        query_part.reshape(steps, seq_rows, heads_local, HD), positions
    ).astype(jnp.bfloat16)
    key_value = key_value.reshape(steps, seq_rows, kv_local, 2, HD)
    new_keys = rotary(key_value[:, :, :, 0], positions).astype(jnp.bfloat16)
    new_values = key_value[:, :, :, 1].astype(jnp.bfloat16)
    attended = attend(
        queries.reshape(steps, seq_rows, kv_local, GROUP, HD).transpose(1, 2, 0, 3, 4),
        key_cache,
        value_cache,
        cache_lengths,
        new_keys.transpose(1, 0, 2, 3),
        new_values.transpose(1, 0, 2, 3),
    )
    attended = attended.transpose(2, 0, 1, 3, 4).reshape(steps * seq_rows, query_cols)
    gathered = gather_rows(attended, n, 1).reshape(steps * seqs, query_cols)
    partial_out = jnp.dot(gathered, out_weight, preferred_element_type=jnp.float32)
    resid = add_residual(partial_out.astype(jnp.bfloat16), current, m, 2)

    values, columns = gained(resid, ffn_gain)
    activated = project(values, columns, [gate_weight, up_weight], n, True, 3)
    gathered = activated.reshape(steps * seqs, hidden)
    partial_down = jnp.dot(gathered, down_weight, preferred_element_type=jnp.float32)
    result = add_residual(partial_down.astype(jnp.bfloat16), resid, m, 5)
    return (
        result.reshape(n, steps, seq_rows, local).transpose(1, 0, 2, 3).reshape(steps, seqs, local)
    )


def solution(mesh):
    in_specs = (
        P(None, None, "gy"),
        P("gy"),
        P("gy", None, "gx", None),
        P("gy", None, "gx", None),
        P("gy"),
        P("gy", "gx"),
        P("gy", "gx"),
        P("gx", "gy"),
        P("gy"),
        P("gy", "gx"),
        P("gy", "gx"),
        P("gx", "gy"),
    )
    out_specs = P(None, None, "gy")
    return jax.shard_map(
        per_device, mesh=mesh, in_specs=in_specs, out_specs=out_specs, check_vma=False
    )
```

```python
import functools
import math

import jax
import jax.numpy as jnp
from jax import lax
from jax.experimental import pallas as pl
from jax.experimental.pallas import tpu as pltpu
from jax.sharding import PartitionSpec as P

HD = 128
GROUP = 8
EXTRA = 128
VMEM_LIMIT = 56 * 1024 * 1024
MESH = pl.DeviceIdType.MESH

epsilon = 1e-05
rotary_base = 500000.0


def remote(src, dst, send, recv, axis, device):
    return pltpu.make_async_remote_copy(
        src_ref=src,
        dst_ref=dst,
        send_sem=send,
        recv_sem=recv,
        device_id={axis: device},
        device_id_type=MESH,
    )


def enter(axis, peers):
    barrier = pltpu.get_barrier_semaphore()
    for peer in peers:
        pl.semaphore_signal(barrier, inc=1, device_id={axis: peer}, device_id_type=MESH)
    pl.semaphore_wait(barrier, len(peers))


def flipped(me, r):
    value = me
    for j in range(r.bit_length()):
        if (r >> j) & 1:
            value = value + (1 << j) * (1 - 2 * lax.rem(me // (1 << j), 2))
    return value


def bit_order(levels, part, parts):
    order = list(range(levels))
    return order[1:] + order[:1] if parts > 3 and part == 0 else order


class Share:
    def __init__(self, me, levels, buf, send_sem, recv_sem):
        self.me, self.levels, self.buf = me, levels, buf
        self.send_sem, self.recv_sem = send_sem, recv_sem
        self.copies, self.bits, self.cols, self.helds = {}, {}, {}, {}

    def send(self, s, step, held, r):
        bit = self.bits[s][step]
        slot = (1 << step) - 1 + held
        block = self.buf.at[flipped(self.me, r), :, self.cols[s]]
        copy = remote(
            block,
            block,
            self.send_sem.at[s, slot],
            self.recv_sem.at[s, slot],
            "gy",
            flipped(self.me, 1 << bit),
        )
        copy.start()
        self.copies[s, step, held] = copy

    def start(self, s, order, cols):
        self.bits[s], self.cols[s] = order[::-1], cols
        self.helds[s] = [0]
        for step in range(self.levels):
            self.send(s, step, 0, 0)

    def next(self, s, step):
        bit = self.bits[s][step]
        held = self.helds[s]
        for j, r in enumerate(list(held)):
            self.copies[s, step, j].wait_recv()
            held.append(r ^ (1 << bit))
            for later in range(step + 1, self.levels):
                self.send(s, later, len(held) - 1, held[-1])

    def end(self):
        for copy in self.copies.values():
            copy.wait_send()


def project_kernel(n, parts, gather, width, x_ref, sq_ref, w1_ref, w2_ref, *refs):
    if gather:
        w3_ref, out_ref, w3, full, dsum, ls, as_, ar = refs[0], refs[1], *refs[-6:]
        refs = refs[2:-6]
    else:
        out1_ref, out2_ref, refs = refs[0], refs[1], refs[2:]
    w1, w2, p_ref, cur, got, scale, ws, ss, rs = refs
    levels = n.bit_length() - 1
    me = lax.axis_index("gy")
    rows = sq_ref.shape[1]
    a, b = w1.shape[1] // parts, w2.shape[1] // parts
    size = a + b
    loads, late_loads = [], []
    for s in range(parts):
        pair = []
        for j, (src, dst, c) in enumerate(((w1_ref, w1, a), (w2_ref, w2, b))):
            cols = pl.ds(s * c, c)
            copy = pltpu.make_async_copy(src.at[:, cols], dst.at[:, cols], ws.at[s, j])
            copy.start()
            pair.append(copy)
        loads.append(pair)
    enter("gy", [flipped(me, 1 << j) for j in range(levels)])
    if gather:
        for s in range(parts):
            lines = pl.ds(s * a, a)
            copy = pltpu.make_async_copy(w3_ref.at[lines], w3.at[lines], ls.at[s])
            copy.start()
            late_loads.append(copy)
        share = Share(me, levels, full, as_, ar)
    segments = [(sq_ref, 0, parts * size, EXTRA)]
    segments += [(p_ref, s * size, s * size, size) for s in range(parts)]
    orders = [list(range(levels))] + [bit_order(levels, s, parts) for s in range(parts)]
    kept, copies = {}, {}
    for g, order in enumerate(orders):
        kept[g, 0] = list(range(n))
        for q, bit in enumerate(order):
            rest = [r for r in kept[g, q] if not (r >> bit) & 1]
            if q + 1 < levels:
                rest.sort(key=lambda r: not (r >> order[q + 1]) & 1)
            kept[g, q + 1] = rest

    def base(q):
        return n - (n >> q)

    def held(g, q, r):
        src, start, place, count = segments[g]
        if q == 0:
            return src, flipped(me, r), pl.ds(start, count)
        return cur, kept[g, 1].index(r), pl.ds(place, count)

    def send(g, q, r):
        bit = orders[g][q]
        place, count = segments[g][2:]
        src, lead, cols = held(g, q, r ^ (1 << bit))
        slot = base(q) + kept[g, q + 1].index(r)
        copy = remote(
            src.at[lead, :, cols],
            got.at[slot, :, pl.ds(place, count)],
            ss.at[g, slot],
            rs.at[g, slot],
            "gy",
            flipped(me, 1 << bit),
        )
        copy.start()
        copies[g, q, r] = copy

    def first(g):
        for r in kept[g, 1]:
            send(g, 0, r)

    def finish(g, q):
        place, count = segments[g][2:]
        for j, r in enumerate(kept[g, q + 1]):
            copies[g, q, r].wait_recv()
            src, lead, cols = held(g, q, r)
            total = src[lead, :, cols].astype(jnp.float32) + got[
                base(q) + j, :, pl.ds(place, count)
            ].astype(jnp.float32)
            if q + 1 < levels:
                cur[kept[g, 1].index(r), :, pl.ds(place, count)] = total.astype(jnp.bfloat16)
                bit = orders[g][q + 1]
                if (r >> bit) & 1:
                    send(g, q + 1, r ^ (1 << bit))
        return total

    first(0)
    for t in range(parts + 1 + 2 * levels):
        if t < parts:
            for copy in loads[t]:
                copy.wait()
            x = x_ref[...]
            for buf, c, skip in ((w1, a, 0), (w2, b, a)):
                dot = jnp.dot(
                    x, buf[:, pl.ds(t * c, c)], preferred_element_type=jnp.float32
                ).astype(jnp.bfloat16)
                p_ref[:, :, pl.ds(t * size + skip, c)] = dot.reshape(n, rows, c)
            first(t + 1)
        if t < levels:
            squares = finish(0, t)
            if t == levels - 1:
                scale[...] = jnp.broadcast_to(
                    lax.rsqrt((squares[:, 0:1] + squares[:, 1:2]) / width + epsilon), scale.shape
                )
        for q in range(levels):
            s = t - 1 - q
            if not 0 <= s < parts:
                continue
            total = finish(s + 1, q)
            if q + 1 < levels:
                continue
            total = total * scale[:, 0:1]
            if gather:
                cols = pl.ds(s * a, a)
                gate, up = total[:, :a], total[:, a:]
                full[me, :, cols] = (gate / (1.0 + jnp.exp(-gate)) * up).astype(jnp.bfloat16)
                share.start(s, orders[s + 1], cols)
            else:
                out1_ref[:, pl.ds(s * a, a)] = total[:, :a]
                out2_ref[:, pl.ds(s * b, b)] = total[:, a:]
        if gather:
            for step in range(levels):
                s = t - 1 - levels - step
                if 0 <= s < parts:
                    share.next(s, step)
                    if step == levels - 1:
                        late_loads[s].wait()
                        add_part(full, w3, dsum, out_ref, s, parts)
    for copy in copies.values():
        copy.wait_send()
    if gather:
        share.end()


def add_part(full, weight, dsum, out_ref, s, parts):
    n, rows, cols = full.shape
    c = cols // parts
    dot = jnp.dot(
        full[:, :, pl.ds(s * c, c)].reshape(n * rows, c),
        weight[pl.ds(s * c, c), :],
        preferred_element_type=jnp.float32,
    )
    if s:
        dot = dsum[...] + dot
    if s + 1 < parts:
        dsum[...] = dot
    else:
        out_ref[...] = dot.astype(jnp.bfloat16)


def project(values, columns, weights, n, collective_id):
    total_rows, depth = values.shape
    rows = total_rows // n
    levels = n.bit_length() - 1
    c1, c2 = weights[0].shape[1], weights[1].shape[1]
    gather = len(weights) == 3
    parts = max(p for p in range(1, 8) if c1 % (128 * p) == 0 and c2 % (128 * p) == 0)
    cols = c1 + c2
    wide = cols + EXTRA
    dma = pltpu.SemaphoreType.DMA
    vmem = pl.BlockSpec(memory_space=pltpu.VMEM)
    if gather:
        local = weights[2].shape[1]
        out_shape = jax.ShapeDtypeStruct((total_rows, local), jnp.bfloat16)
        out_specs = vmem
        more = [
            pltpu.VMEM((c1, local), jnp.bfloat16),
            pltpu.VMEM((n, rows, c1), jnp.bfloat16),
            pltpu.VMEM((total_rows, local), jnp.float32),
            dma((parts,)),
            dma((parts, n - 1)),
            dma((parts, n - 1)),
        ]
    else:
        out_shape = [jax.ShapeDtypeStruct((rows, c), jnp.float32) for c in (c1, c2)]
        out_specs = [vmem] * 2
        more = []
    return pl.pallas_call(
        functools.partial(project_kernel, n, parts, gather, depth * n),
        out_shape=out_shape,
        in_specs=[vmem] * 2 + [pl.BlockSpec(memory_space=pl.ANY)] * len(weights),
        out_specs=out_specs,
        scratch_shapes=[
            pltpu.VMEM((depth, c1), jnp.bfloat16),
            pltpu.VMEM((depth, c2), jnp.bfloat16),
            pltpu.VMEM((n, rows, cols), jnp.bfloat16),
            pltpu.VMEM((n // 2, rows, wide), jnp.bfloat16),
            pltpu.VMEM((n - 1, rows, wide), jnp.bfloat16),
            pltpu.VMEM((rows, 128), jnp.float32),
            dma((parts, 2)),
            dma((parts + 1, n - 1)),
            dma((parts + 1, n - 1)),
        ]
        + more,
        compiler_params=pltpu.CompilerParams(
            collective_id=collective_id, has_side_effects=True, vmem_limit_bytes=VMEM_LIMIT
        ),
        cost_estimate=pl.CostEstimate(
            flops=2 * total_rows * depth * cols, bytes_accessed=2 * depth * cols, transcendentals=0
        ),
    )(values, columns.reshape(n, rows, EXTRA), *weights)


def gather_kernel(n, parts, a_ref, w_ref, out_ref, w, full, dsum, ls, as_, ar):
    levels = n.bit_length() - 1
    me = lax.axis_index("gy")
    c = a_ref.shape[1] // parts
    loads = []
    for s in range(parts):
        lines = pl.ds(s * c, c)
        copy = pltpu.make_async_copy(w_ref.at[lines], w.at[lines], ls.at[s])
        copy.start()
        loads.append(copy)
    full[me] = a_ref[...]
    enter("gy", [flipped(me, 1 << j) for j in range(levels)])
    share = Share(me, levels, full, as_, ar)
    for s in range(parts):
        share.start(s, bit_order(levels, s, parts), pl.ds(s * c, c))
    for t in range(parts + levels - 1):
        for step in range(levels):
            s = t - step
            if 0 <= s < parts:
                share.next(s, step)
                if step == levels - 1:
                    loads[s].wait()
                    add_part(full, w, dsum, out_ref, s, parts)
    share.end()


def gather_project(block, weight, n, collective_id):
    rows, cols = block.shape
    local = weight.shape[1]
    parts = max(p for p in range(1, 5) if cols % (128 * p) == 0)
    dma = pltpu.SemaphoreType.DMA
    vmem = pl.BlockSpec(memory_space=pltpu.VMEM)
    return pl.pallas_call(
        functools.partial(gather_kernel, n, parts),
        out_shape=jax.ShapeDtypeStruct((n * rows, local), jnp.bfloat16),
        in_specs=[vmem, pl.BlockSpec(memory_space=pl.ANY)],
        out_specs=vmem,
        scratch_shapes=[
            pltpu.VMEM((cols, local), jnp.bfloat16),
            pltpu.VMEM((n, rows, cols), jnp.bfloat16),
            pltpu.VMEM((n * rows, local), jnp.float32),
            dma((parts,)),
            dma((parts, n - 1)),
            dma((parts, n - 1)),
        ],
        compiler_params=pltpu.CompilerParams(
            collective_id=collective_id, has_side_effects=True, vmem_limit_bytes=VMEM_LIMIT
        ),
    )(block, weight)


def residual_kernel(n, p_ref, base_ref, out_ref, near, going, far, *sems):
    ns, nr, fs, fr, as_, ar, bs, br = sems
    outer = n // 2
    me = lax.axis_index("gx")
    o, i = me // 2, lax.rem(me, 2)
    partner = me + 1 - 2 * i
    across = [lax.rem(o + k, outer) for k in range(outer)]
    behind = [lax.rem(o + outer - k, outer) * 2 + i for k in range(outer)]
    enter("gx", [partner] + [across[k] * 2 + i for k in range(1, outer)])
    order = [(k + 1) % outer for k in range(outer)]
    copies, near_copies, far_copies, share_far, share_near = [], {}, {}, {}, {}

    def send(src, dst, send_sem, recv_sem, device):
        copy = remote(src, dst, send_sem, recv_sem, "gx", device)
        copy.start()
        copies.append(copy)
        return copy

    for k in order:
        near_copies[k] = send(
            p_ref.at[across[k] * 2 + 1 - i], near.at[k], ns.at[k], nr.at[k], partner
        )
    for k in order:
        near_copies[k].wait_recv()
        total = p_ref[across[k] * 2 + i].astype(jnp.float32) + near[k].astype(jnp.float32)
        if k:
            going[k - 1] = total.astype(jnp.bfloat16)
            far_copies[k] = send(
                going.at[k - 1],
                far.at[k - 1],
                fs.at[k - 1],
                fr.at[k - 1],
                across[k] * 2 + i,
            )
    for k in range(1, outer):
        far_copies[k].wait_recv()
        total = total + far[k - 1].astype(jnp.float32)
    out_ref[me] = (base_ref[me].astype(jnp.float32) + total).astype(jnp.bfloat16)
    block = out_ref.at[me]
    for k in range(1, outer):
        share_far[k] = send(block, block, as_.at[k - 1], ar.at[k - 1], across[k] * 2 + i)
    share_near[0] = send(block, block, bs.at[0], br.at[0], partner)
    for k in range(1, outer):
        share_far[k].wait_recv()
        block = out_ref.at[behind[k]]
        share_near[k] = send(block, block, bs.at[k], br.at[k], partner)
    for copy in share_near.values():
        copy.wait_recv()
    for copy in copies:
        copy.wait_send()


def add_residual(partial, base, n, collective_id):
    rows, cols = partial.shape
    shape = (n, rows // n, cols)
    outer = n // 2
    dma = pltpu.SemaphoreType.DMA
    result = pl.pallas_call(
        functools.partial(residual_kernel, n),
        out_shape=jax.ShapeDtypeStruct(shape, jnp.bfloat16),
        in_specs=[pl.BlockSpec(memory_space=pltpu.VMEM)] * 2,
        out_specs=pl.BlockSpec(memory_space=pltpu.VMEM),
        scratch_shapes=[
            pltpu.VMEM((outer,) + shape[1:], jnp.bfloat16),
            pltpu.VMEM((outer - 1,) + shape[1:], jnp.bfloat16),
            pltpu.VMEM((outer - 1,) + shape[1:], jnp.bfloat16),
        ]
        + [dma((outer,))] * 2
        + [dma((outer - 1,))] * 4
        + [dma((outer,))] * 2,
        compiler_params=pltpu.CompilerParams(
            collective_id=collective_id, has_side_effects=True, vmem_limit_bytes=VMEM_LIMIT
        ),
    )(partial.reshape(shape), base.reshape(shape))
    return result.reshape(rows, cols)


def rotary(values, positions):
    half_dim = HD // 2
    inv_freq = rotary_base ** (-(jnp.arange(half_dim, dtype=jnp.float32) * 2.0 / HD))
    angles = positions[..., None] * inv_freq
    cosine = jnp.cos(angles)[..., None, :]
    sine_part = jnp.sin(angles)[..., None, :]
    first_half = values[..., :half_dim]
    second_half = values[..., half_dim:]
    return jnp.concatenate(
        [
            first_half * cosine - second_half * sine_part,
            second_half * cosine + first_half * sine_part,
        ],
        axis=-1,
    )


def attend(queries, cached_keys, cached_values, lengths, extra_keys, extra_values):
    seqs, kv, steps = queries.shape[:3]
    flat = queries.reshape(seqs, kv, steps * GROUP, HD)
    scale_factor = 1.0 / math.sqrt(HD)
    cached = (
        jnp.einsum("sgjd,stgd->sgjt", flat, cached_keys, preferred_element_type=jnp.float32)
        * scale_factor
    )
    valid = jnp.arange(cached_keys.shape[1])[None, :] < lengths[:, None]
    cached = jnp.where(valid[:, None, None, :], cached, -1e30)
    recent = (
        jnp.einsum("sgjd,segd->sgje", flat, extra_keys, preferred_element_type=jnp.float32)
        * scale_factor
    )
    step_of = jnp.arange(steps * GROUP) // GROUP
    seen = jnp.arange(steps)[None, :] <= step_of[:, None]
    recent = jnp.where(seen[None, None], recent, -1e30)
    highest = jnp.maximum(
        jnp.max(cached, axis=-1, keepdims=True), jnp.max(recent, axis=-1, keepdims=True)
    )
    cached_exp = jnp.exp(cached - highest)
    recent_exp = jnp.exp(recent - highest)
    totals = jnp.sum(cached_exp, axis=-1, keepdims=True) + jnp.sum(
        recent_exp, axis=-1, keepdims=True
    )
    cached_probs = (cached_exp / totals).astype(jnp.bfloat16)
    recent_probs = (recent_exp / totals).astype(jnp.bfloat16)
    mixed = jnp.einsum(
        "sgjt,stgd->sgjd", cached_probs, cached_values, preferred_element_type=jnp.float32
    )
    mixed = mixed + jnp.einsum(
        "sgje,segd->sgjd", recent_probs, extra_values, preferred_element_type=jnp.float32
    )
    return mixed.reshape(seqs, kv, steps, GROUP, HD).astype(jnp.bfloat16)


def gained(values, gain):
    wide = values.astype(jnp.float32)
    squares = jnp.sum(wide * wide, axis=1, keepdims=True)
    high = squares.astype(jnp.bfloat16)
    low = (squares - high.astype(jnp.float32)).astype(jnp.bfloat16)
    pad = jnp.zeros((values.shape[0], EXTRA - 2), jnp.bfloat16)
    return (wide * gain.astype(jnp.float32)).astype(jnp.bfloat16), jnp.concatenate(
        [high, low, pad], axis=1
    )


def per_device(
    tokens,
    cache_lengths,
    key_cache,
    value_cache,
    attn_gain,
    query_weight,
    keyval_weight,
    out_weight,
    ffn_gain,
    gate_weight,
    up_weight,
    down_weight,
):
    n, m = lax.axis_size("gy"), lax.axis_size("gx")
    steps, seqs, local = tokens.shape
    seq_rows = cache_lengths.shape[0]
    query_cols = query_weight.shape[1]
    heads_local = query_cols // HD
    kv_local = keyval_weight.shape[1] // (2 * HD)

    current = (
        tokens.reshape(steps, n, seq_rows, local).transpose(1, 0, 2, 3).reshape(steps * seqs, local)
    )
    values, columns = gained(current, attn_gain)
    query_part, key_value = project(values, columns, [query_weight, keyval_weight], n, 0)
    positions = (cache_lengths[None, :] + jnp.arange(steps)[:, None]).astype(jnp.float32)
    queries = rotary(
        query_part.reshape(steps, seq_rows, heads_local, HD), positions
    ).astype(jnp.bfloat16)
    key_value = key_value.reshape(steps, seq_rows, kv_local, 2, HD)
    new_keys = rotary(key_value[:, :, :, 0], positions).astype(jnp.bfloat16)
    new_values = key_value[:, :, :, 1].astype(jnp.bfloat16)
    attended = attend(
        queries.reshape(steps, seq_rows, kv_local, GROUP, HD).transpose(1, 2, 0, 3, 4),
        key_cache,
        value_cache,
        cache_lengths,
        new_keys.transpose(1, 0, 2, 3),
        new_values.transpose(1, 0, 2, 3),
    )
    attended = attended.transpose(2, 0, 1, 3, 4).reshape(steps * seq_rows, query_cols)
    partial_out = gather_project(attended, out_weight, n, 1)
    resid = add_residual(partial_out, current, m, 2)

    values, columns = gained(resid, ffn_gain)
    partial_down = project(values, columns, [gate_weight, up_weight, down_weight], n, 3)
    result = add_residual(partial_down, resid, m, 5)
    return (
        result.reshape(n, steps, seq_rows, local).transpose(1, 0, 2, 3).reshape(steps, seqs, local)
    )


def solution(mesh):
    in_specs = (
        P(None, None, "gy"),
        P("gy"),
        P("gy", None, "gx", None),
        P("gy", None, "gx", None),
        P("gy"),
        P("gy", "gx"),
        P("gy", "gx"),
        P("gx", "gy"),
        P("gy"),
        P("gy", "gx"),
        P("gy", "gx"),
        P("gx", "gy"),
    )
    out_specs = P(None, None, "gy")
    return jax.shard_map(
        per_device, mesh=mesh, in_specs=in_specs, out_specs=out_specs, check_vma=False
    )
```

```python
import functools
import math

import jax
import jax.numpy as jnp
from jax import lax
from jax.experimental import pallas as pl
from jax.experimental.pallas import tpu as pltpu
from jax.sharding import PartitionSpec as P

HD = 128
GROUP = 8
EXTRA = 128
HALVES = 2
VMEM_LIMIT = 56 * 1024 * 1024
MESH = pl.DeviceIdType.MESH

epsilon = 1e-05
rotary_base = 500000.0


def remote(src, dst, send, recv, axis, device):
    return pltpu.make_async_remote_copy(
        src_ref=src,
        dst_ref=dst,
        send_sem=send,
        recv_sem=recv,
        device_id={axis: device},
        device_id_type=MESH,
    )


def enter(axis, peers):
    barrier = pltpu.get_barrier_semaphore()
    for peer in peers:
        pl.semaphore_signal(barrier, inc=1, device_id={axis: peer}, device_id_type=MESH)
    pl.semaphore_wait(barrier, len(peers))


def flipped(me, r):
    value = me
    for j in range(r.bit_length()):
        if (r >> j) & 1:
            value = value + (1 << j) * (1 - 2 * lax.rem(me // (1 << j), 2))
    return value


def bit_order(levels, part, parts):
    order = list(range(levels))
    return order[1:] + order[:1] if parts > 3 and part == 0 else order


class Share:
    def __init__(self, me, levels, buf, send_sem, recv_sem):
        self.me, self.levels, self.buf = me, levels, buf
        self.send_sem, self.recv_sem = send_sem, recv_sem
        self.copies, self.bits, self.cols, self.helds = {}, {}, {}, {}

    def send(self, s, step, held, r):
        bit = self.bits[s][step]
        slot = (1 << step) - 1 + held
        block = self.buf.at[flipped(self.me, r), :, self.cols[s]]
        copy = remote(
            block,
            block,
            self.send_sem.at[s, slot],
            self.recv_sem.at[s, slot],
            "gy",
            flipped(self.me, 1 << bit),
        )
        copy.start()
        self.copies[s, step, held] = copy

    def start(self, s, order, cols):
        self.bits[s], self.cols[s] = order[::-1], cols
        self.helds[s] = [0]
        for step in range(self.levels):
            self.send(s, step, 0, 0)

    def next(self, s, step):
        bit = self.bits[s][step]
        held = self.helds[s]
        for j, r in enumerate(list(held)):
            self.copies[s, step, j].wait_recv()
            held.append(r ^ (1 << bit))
            for later in range(step + 1, self.levels):
                self.send(s, later, len(held) - 1, held[-1])

    def end(self):
        for copy in self.copies.values():
            copy.wait_send()


def project_kernel(n, parts, gather, width, v_ref, gain_ref, w1_ref, w2_ref, *refs):
    if gather:
        w3_ref, out_ref, w3, full, dsum, ls, as_, ar = refs[0], refs[1], *refs[-6:]
        refs = refs[2:-6]
    else:
        out1_ref, out2_ref, refs = refs[0], refs[1], refs[2:]
    w1, w2, x_ref, sq_ref, p_ref, cur, got, scale, ws, ss, rs = refs
    levels = n.bit_length() - 1
    me = lax.axis_index("gy")
    rows = v_ref.shape[0] // n
    a, b = w1.shape[1] // parts, w2.shape[1] // parts
    size = a + b
    loads, late_loads = [], []
    for s in range(parts):
        pair = []
        for j, (src, dst, c) in enumerate(((w1_ref, w1, a), (w2_ref, w2, b))):
            cols = pl.ds(s * c, c)
            copy = pltpu.make_async_copy(src.at[:, cols], dst.at[:, cols], ws.at[s, j])
            copy.start()
            pair.append(copy)
        loads.append(pair)
    enter("gy", [flipped(me, 1 << j) for j in range(levels)])
    if gather:
        for s in range(parts):
            lines = pl.ds(s * a, a)
            copy = pltpu.make_async_copy(w3_ref.at[lines], w3.at[lines], ls.at[s])
            copy.start()
            late_loads.append(copy)
        share = Share(me, levels, full, as_, ar)
    values = v_ref[...].astype(jnp.float32)
    x_ref[...] = (values * gain_ref[...]).astype(jnp.bfloat16)
    squares = jnp.sum(values * values, axis=1, keepdims=True)
    high = squares.astype(jnp.bfloat16).astype(jnp.float32)
    lane = lax.broadcasted_iota(jnp.int32, (n * rows, EXTRA), 1)
    columns = jnp.where(lane == 0, high, jnp.where(lane == 1, squares - high, 0.0))
    sq_ref[...] = columns.astype(jnp.bfloat16).reshape(n, rows, EXTRA)
    segments = [(sq_ref, 0, parts * size, EXTRA)]
    segments += [(p_ref, s * size, s * size, size) for s in range(parts)]
    orders = [list(range(levels))] + [bit_order(levels, s, parts) for s in range(parts)]
    kept, copies = {}, {}
    for g, order in enumerate(orders):
        kept[g, 0] = list(range(n))
        for q, bit in enumerate(order):
            rest = [r for r in kept[g, q] if not (r >> bit) & 1]
            if q + 1 < levels:
                rest.sort(key=lambda r: not (r >> order[q + 1]) & 1)
            kept[g, q + 1] = rest

    def base(q):
        return n - (n >> q)

    def held(g, q, r):
        src, start, place, count = segments[g]
        if q == 0:
            return src, flipped(me, r), pl.ds(start, count)
        return cur, kept[g, 1].index(r), pl.ds(place, count)

    def send(g, q, r):
        bit = orders[g][q]
        place, count = segments[g][2:]
        src, lead, cols = held(g, q, r ^ (1 << bit))
        slot = base(q) + kept[g, q + 1].index(r)
        copy = remote(
            src.at[lead, :, cols],
            got.at[slot, :, pl.ds(place, count)],
            ss.at[g, slot],
            rs.at[g, slot],
            "gy",
            flipped(me, 1 << bit),
        )
        copy.start()
        copies[g, q, r] = copy

    def first(g):
        for r in kept[g, 1]:
            send(g, 0, r)

    def finish(g, q):
        place, count = segments[g][2:]
        for j, r in enumerate(kept[g, q + 1]):
            copies[g, q, r].wait_recv()
            src, lead, cols = held(g, q, r)
            total = src[lead, :, cols].astype(jnp.float32) + got[
                base(q) + j, :, pl.ds(place, count)
            ].astype(jnp.float32)
            if q + 1 < levels:
                cur[kept[g, 1].index(r), :, pl.ds(place, count)] = total.astype(jnp.bfloat16)
                bit = orders[g][q + 1]
                if (r >> bit) & 1:
                    send(g, q + 1, r ^ (1 << bit))
        return total

    first(0)
    for t in range(parts + 1 + 2 * levels):
        if t < parts:
            for copy in loads[t]:
                copy.wait()
            x = x_ref[...]
            for buf, c, skip in ((w1, a, 0), (w2, b, a)):
                dot = jnp.dot(
                    x, buf[:, pl.ds(t * c, c)], preferred_element_type=jnp.float32
                ).astype(jnp.bfloat16)
                p_ref[:, :, pl.ds(t * size + skip, c)] = dot.reshape(n, rows, c)
            first(t + 1)
        if t < levels:
            squares = finish(0, t)
            if t == levels - 1:
                scale[...] = jnp.broadcast_to(
                    lax.rsqrt((squares[:, 0:1] + squares[:, 1:2]) / width + epsilon), scale.shape
                )
        for q in range(levels):
            s = t - 1 - q
            if not 0 <= s < parts:
                continue
            total = finish(s + 1, q)
            if q + 1 < levels:
                continue
            total = total * scale[:, 0:1]
            if gather:
                cols = pl.ds(s * a, a)
                gate, up = total[:, :a], total[:, a:]
                full[me, :, cols] = (gate / (1.0 + jnp.exp(-gate)) * up).astype(jnp.bfloat16)
                share.start(s, orders[s + 1], cols)
            else:
                out1_ref[:, pl.ds(s * a, a)] = total[:, :a]
                out2_ref[:, pl.ds(s * b, b)] = total[:, a:]
        if gather:
            for step in range(levels):
                s = t - 1 - levels - step
                if 0 <= s < parts:
                    share.next(s, step)
                    if step == levels - 1:
                        late_loads[s].wait()
                        add_part(full, w3, dsum, out_ref, s, parts)
    for copy in copies.values():
        copy.wait_send()
    if gather:
        share.end()


def add_part(full, weight, dsum, out_ref, s, parts):
    n, rows, cols = full.shape
    c = cols // parts
    dot = jnp.dot(
        full[:, :, pl.ds(s * c, c)].reshape(n * rows, c),
        weight[pl.ds(s * c, c), :],
        preferred_element_type=jnp.float32,
    )
    if s:
        dot = dsum[...] + dot
    if s + 1 < parts:
        dsum[...] = dot
    else:
        out_ref[...] = dot.astype(jnp.bfloat16)


def project(values, gain, weights, n, collective_id):
    total_rows, depth = values.shape
    rows = total_rows // n
    levels = n.bit_length() - 1
    c1, c2 = weights[0].shape[1], weights[1].shape[1]
    gather = len(weights) == 3
    parts = max(p for p in range(1, 8) if c1 % (128 * p) == 0 and c2 % (128 * p) == 0)
    cols = c1 + c2
    wide = cols + EXTRA
    dma = pltpu.SemaphoreType.DMA
    vmem = pl.BlockSpec(memory_space=pltpu.VMEM)
    if gather:
        local = weights[2].shape[1]
        out_shape = jax.ShapeDtypeStruct((total_rows, local), jnp.bfloat16)
        out_specs = vmem
        more = [
            pltpu.VMEM((c1, local), jnp.bfloat16),
            pltpu.VMEM((n, rows, c1), jnp.bfloat16),
            pltpu.VMEM((total_rows, local), jnp.float32),
            dma((parts,)),
            dma((parts, n - 1)),
            dma((parts, n - 1)),
        ]
    else:
        out_shape = [jax.ShapeDtypeStruct((rows, c), jnp.float32) for c in (c1, c2)]
        out_specs = [vmem] * 2
        more = []
    return pl.pallas_call(
        functools.partial(project_kernel, n, parts, gather, depth * n),
        out_shape=out_shape,
        in_specs=[vmem] * 2 + [pl.BlockSpec(memory_space=pl.ANY)] * len(weights),
        out_specs=out_specs,
        scratch_shapes=[
            pltpu.VMEM((depth, c1), jnp.bfloat16),
            pltpu.VMEM((depth, c2), jnp.bfloat16),
            pltpu.VMEM((total_rows, depth), jnp.bfloat16),
            pltpu.VMEM((n, rows, EXTRA), jnp.bfloat16),
            pltpu.VMEM((n, rows, cols), jnp.bfloat16),
            pltpu.VMEM((n // 2, rows, wide), jnp.bfloat16),
            pltpu.VMEM((n - 1, rows, wide), jnp.bfloat16),
            pltpu.VMEM((rows, 128), jnp.float32),
            dma((parts, 2)),
            dma((parts + 1, n - 1)),
            dma((parts + 1, n - 1)),
        ]
        + more,
        compiler_params=pltpu.CompilerParams(
            collective_id=collective_id, has_side_effects=True, vmem_limit_bytes=VMEM_LIMIT
        ),
        cost_estimate=pl.CostEstimate(
            flops=2 * total_rows * depth * cols, bytes_accessed=2 * depth * cols, transcendentals=0
        ),
    )(values, gain.astype(jnp.float32).reshape(1, depth), *weights)


def gather_kernel(n, parts, a_ref, w_ref, out_ref, w, full, dsum, ls, as_, ar):
    levels = n.bit_length() - 1
    me = lax.axis_index("gy")
    c = a_ref.shape[1] // parts
    loads = []
    for s in range(parts):
        lines = pl.ds(s * c, c)
        copy = pltpu.make_async_copy(w_ref.at[lines], w.at[lines], ls.at[s])
        copy.start()
        loads.append(copy)
    full[me] = a_ref[...]
    enter("gy", [flipped(me, 1 << j) for j in range(levels)])
    share = Share(me, levels, full, as_, ar)
    for s in range(parts):
        share.start(s, bit_order(levels, s, parts), pl.ds(s * c, c))
    for t in range(parts + levels - 1):
        for step in range(levels):
            s = t - step
            if 0 <= s < parts:
                share.next(s, step)
                if step == levels - 1:
                    loads[s].wait()
                    add_part(full, w, dsum, out_ref, s, parts)
    share.end()


def gather_project(block, weight, n, collective_id):
    rows, cols = block.shape
    local = weight.shape[1]
    parts = max(p for p in range(1, 5) if cols % (128 * p) == 0)
    dma = pltpu.SemaphoreType.DMA
    vmem = pl.BlockSpec(memory_space=pltpu.VMEM)
    return pl.pallas_call(
        functools.partial(gather_kernel, n, parts),
        out_shape=jax.ShapeDtypeStruct((n * rows, local), jnp.bfloat16),
        in_specs=[vmem, pl.BlockSpec(memory_space=pl.ANY)],
        out_specs=vmem,
        scratch_shapes=[
            pltpu.VMEM((cols, local), jnp.bfloat16),
            pltpu.VMEM((n, rows, cols), jnp.bfloat16),
            pltpu.VMEM((n * rows, local), jnp.float32),
            dma((parts,)),
            dma((parts, n - 1)),
            dma((parts, n - 1)),
        ],
        compiler_params=pltpu.CompilerParams(
            collective_id=collective_id, has_side_effects=True, vmem_limit_bytes=VMEM_LIMIT
        ),
    )(block, weight)


def residual_kernel(n, p_ref, base_ref, out_ref, near, going, far, *sems):
    ns, nr, fs, fr, as_, ar, bs, br = sems
    outer = n // 2
    me = lax.axis_index("gx")
    o, i = me // 2, lax.rem(me, 2)
    partner = me + 1 - 2 * i
    across = [lax.rem(o + k, outer) for k in range(outer)]
    behind = [lax.rem(o + outer - k, outer) * 2 + i for k in range(outer)]
    enter("gx", [partner] + [across[k] * 2 + i for k in range(1, outer)])
    order = [(k + 1) % outer for k in range(outer)]
    copies, near_copies, far_copies, share_far, share_near = [], {}, {}, {}, {}
    width = p_ref.shape[2] // HALVES
    spans = [pl.ds(h * width, width) for h in range(HALVES)]
    own = {}

    def send(src, dst, send_sem, recv_sem, device):
        copy = remote(src, dst, send_sem, recv_sem, "gx", device)
        copy.start()
        copies.append(copy)
        return copy

    for h, cols in enumerate(spans):
        for k in order:
            near_copies[h, k] = send(
                p_ref.at[across[k] * 2 + 1 - i, :, cols],
                near.at[k, :, cols],
                ns.at[h, k],
                nr.at[h, k],
                partner,
            )
    for h, cols in enumerate(spans):
        for k in order:
            near_copies[h, k].wait_recv()
            total = p_ref[across[k] * 2 + i, :, cols].astype(jnp.float32) + near[
                k, :, cols
            ].astype(jnp.float32)
            if k:
                going[k - 1, :, cols] = total.astype(jnp.bfloat16)
                far_copies[h, k] = send(
                    going.at[k - 1, :, cols],
                    far.at[k - 1, :, cols],
                    fs.at[h, k - 1],
                    fr.at[h, k - 1],
                    across[k] * 2 + i,
                )
            else:
                own[h] = total + base_ref[me, :, cols].astype(jnp.float32)
    for h, cols in enumerate(spans):
        total = own[h]
        for k in range(1, outer):
            far_copies[h, k].wait_recv()
            total = total + far[k - 1, :, cols].astype(jnp.float32)
        out_ref[me, :, cols] = total.astype(jnp.bfloat16)
        block = out_ref.at[me, :, cols]
        for k in range(1, outer):
            share_far[h, k] = send(
                block, block, as_.at[h, k - 1], ar.at[h, k - 1], across[k] * 2 + i
            )
        share_near[h, 0] = send(block, block, bs.at[h, 0], br.at[h, 0], partner)
    for h, cols in enumerate(spans):
        for k in range(1, outer):
            share_far[h, k].wait_recv()
            block = out_ref.at[behind[k], :, cols]
            share_near[h, k] = send(block, block, bs.at[h, k], br.at[h, k], partner)
    for copy in share_near.values():
        copy.wait_recv()
    for copy in copies:
        copy.wait_send()


def add_residual(partial, base, n, collective_id):
    rows, cols = partial.shape
    shape = (n, rows // n, cols)
    outer = n // 2
    dma = pltpu.SemaphoreType.DMA
    result = pl.pallas_call(
        functools.partial(residual_kernel, n),
        out_shape=jax.ShapeDtypeStruct(shape, jnp.bfloat16),
        in_specs=[pl.BlockSpec(memory_space=pltpu.VMEM)] * 2,
        out_specs=pl.BlockSpec(memory_space=pltpu.VMEM),
        scratch_shapes=[
            pltpu.VMEM((outer,) + shape[1:], jnp.bfloat16),
            pltpu.VMEM((outer - 1,) + shape[1:], jnp.bfloat16),
            pltpu.VMEM((outer - 1,) + shape[1:], jnp.bfloat16),
        ]
        + [dma((HALVES, outer))] * 2
        + [dma((HALVES, outer - 1))] * 4
        + [dma((HALVES, outer))] * 2,
        compiler_params=pltpu.CompilerParams(
            collective_id=collective_id, has_side_effects=True, vmem_limit_bytes=VMEM_LIMIT
        ),
    )(partial.reshape(shape), base.reshape(shape))
    return result.reshape(rows, cols)


def rotary(values, positions):
    half_dim = HD // 2
    inv_freq = rotary_base ** (-(jnp.arange(half_dim, dtype=jnp.float32) * 2.0 / HD))
    angles = positions[..., None] * inv_freq
    cosine = jnp.cos(angles)[..., None, :]
    sine_part = jnp.sin(angles)[..., None, :]
    first_half = values[..., :half_dim]
    second_half = values[..., half_dim:]
    return jnp.concatenate(
        [
            first_half * cosine - second_half * sine_part,
            second_half * cosine + first_half * sine_part,
        ],
        axis=-1,
    )


def attend(queries, cached_keys, cached_values, lengths, extra_keys, extra_values):
    seqs, kv, steps = queries.shape[:3]
    flat = queries.reshape(seqs, kv, steps * GROUP, HD)
    scale_factor = 1.0 / math.sqrt(HD)
    cached = (
        jnp.einsum("sgjd,stgd->sgjt", flat, cached_keys, preferred_element_type=jnp.float32)
        * scale_factor
    )
    valid = jnp.arange(cached_keys.shape[1])[None, :] < lengths[:, None]
    cached = jnp.where(valid[:, None, None, :], cached, -1e30)
    recent = (
        jnp.einsum("sgjd,segd->sgje", flat, extra_keys, preferred_element_type=jnp.float32)
        * scale_factor
    )
    step_of = jnp.arange(steps * GROUP) // GROUP
    seen = jnp.arange(steps)[None, :] <= step_of[:, None]
    recent = jnp.where(seen[None, None], recent, -1e30)
    highest = jnp.maximum(
        jnp.max(cached, axis=-1, keepdims=True), jnp.max(recent, axis=-1, keepdims=True)
    )
    cached_exp = jnp.exp(cached - highest)
    recent_exp = jnp.exp(recent - highest)
    totals = jnp.sum(cached_exp, axis=-1, keepdims=True) + jnp.sum(
        recent_exp, axis=-1, keepdims=True
    )
    cached_probs = (cached_exp / totals).astype(jnp.bfloat16)
    recent_probs = (recent_exp / totals).astype(jnp.bfloat16)
    mixed = jnp.einsum(
        "sgjt,stgd->sgjd", cached_probs, cached_values, preferred_element_type=jnp.float32
    )
    mixed = mixed + jnp.einsum(
        "sgje,segd->sgjd", recent_probs, extra_values, preferred_element_type=jnp.float32
    )
    return mixed.reshape(seqs, kv, steps, GROUP, HD).astype(jnp.bfloat16)


def per_device(
    tokens,
    cache_lengths,
    key_cache,
    value_cache,
    attn_gain,
    query_weight,
    keyval_weight,
    out_weight,
    ffn_gain,
    gate_weight,
    up_weight,
    down_weight,
):
    n, m = lax.axis_size("gy"), lax.axis_size("gx")
    steps, seqs, local = tokens.shape
    seq_rows = cache_lengths.shape[0]
    query_cols = query_weight.shape[1]
    heads_local = query_cols // HD
    kv_local = keyval_weight.shape[1] // (2 * HD)

    current = (
        tokens.reshape(steps, n, seq_rows, local).transpose(1, 0, 2, 3).reshape(steps * seqs, local)
    )
    query_part, key_value = project(current, attn_gain, [query_weight, keyval_weight], n, 0)
    positions = (cache_lengths[None, :] + jnp.arange(steps)[:, None]).astype(jnp.float32)
    queries = rotary(
        query_part.reshape(steps, seq_rows, heads_local, HD), positions
    ).astype(jnp.bfloat16)
    key_value = key_value.reshape(steps, seq_rows, kv_local, 2, HD)
    new_keys = rotary(key_value[:, :, :, 0], positions).astype(jnp.bfloat16)
    new_values = key_value[:, :, :, 1].astype(jnp.bfloat16)
    attended = attend(
        queries.reshape(steps, seq_rows, kv_local, GROUP, HD).transpose(1, 2, 0, 3, 4),
        key_cache,
        value_cache,
        cache_lengths,
        new_keys.transpose(1, 0, 2, 3),
        new_values.transpose(1, 0, 2, 3),
    )
    attended = attended.transpose(2, 0, 1, 3, 4).reshape(steps * seq_rows, query_cols)
    partial_out = gather_project(attended, out_weight, n, 1)
    resid = add_residual(partial_out, current, m, 2)

    partial_down = project(resid, ffn_gain, [gate_weight, up_weight, down_weight], n, 3)
    result = add_residual(partial_down, resid, m, 5)
    return (
        result.reshape(n, steps, seq_rows, local).transpose(1, 0, 2, 3).reshape(steps, seqs, local)
    )


def solution(mesh):
    in_specs = (
        P(None, None, "gy"),
        P("gy"),
        P("gy", None, "gx", None),
        P("gy", None, "gx", None),
        P("gy"),
        P("gy", "gx"),
        P("gy", "gx"),
        P("gx", "gy"),
        P("gy"),
        P("gy", "gx"),
        P("gy", "gx"),
        P("gx", "gy"),
    )
    out_specs = P(None, None, "gy")
    return jax.shard_map(
        per_device, mesh=mesh, in_specs=in_specs, out_specs=out_specs, check_vma=False
    )
```
